32 devices in a mesh: groups: 2 (over y), dp: 4 (over z), mp: 4 (over x, core).
Axes of the slice: x: 2, y: 2, z: 4, core: 2. Of those that a mesh axis runs over, the one named last changes fastest.
Arguments:
- replay_obs: bfloat16 [256, 16, 2048], P(('groups', 'dp'), None, 'mp'), parts along dimension 0, may hold values from -6 to 6
- priorities: int32 [256], P(('groups', 'dp')), parts along dimension 0, may hold values from 16 to 191, as said below
- sample_owner: int32 [256, 1], P(('groups', 'dp')), parts along dimension 0, may hold values from 0 to 3; in each aligned block of 32 rows (0 to 31, 32 to 63, ...) at most 16 rows name the same one
- sample_slot: int32 [256], P(('groups', 'dp')), parts along dimension 0, may hold values from 0 to 31
- cotangent: bfloat16 [4096, 2048], P(('groups', 'dp'), 'mp'), parts along dimension 0, may hold values from -0.39648438 to 0.39648438
- norm_gain: float32 [2048], replicated, may hold values from 0.5 to 1.5
- w_in: bfloat16 [2048, 4096], P(None, 'mp'), may hold values from -0.125 to 0.125
- w_out: bfloat16 [2048, 4096], P(None, 'mp'), may hold values from -0.09375 to 0.09375
Outputs:
- grad_in: bfloat16 [4096, 4096], P(('groups', 'dp'), 'mp'), parts along dimension 0
- grad_out: bfloat16 [4096, 4096], P(('groups', 'dp'), 'mp'), parts along dimension 0
The draws below stay inside these ranges and needn't reach their ends.
There are 2 independent parts, one for each index of `groups`. The reference program is written for one: setup_inputs(seed, part) draws one part's arguments, and reference() takes and returns one part's arrays. A program takes and returns all parts, laid end to end along the dimension named above; an argument that names none is the same for every part. Nothing has to cross between parts.
Inputs may be any that keep to these rules, and one draw needn't show every extreme that they name: `sample_owner`: within the 32 samples of one learner no replay shard is named more than 16 times; in every draw some learner names one shard exactly 16 times. `priorities`: priorities are whole numbers; the smallest and the largest stated are reached in every draw.
All inputs are finite; a program needn't handle non-finite values.
Results may differ from the reference program's by a relative error of at most 0.012.
Values may be sent and summed in bfloat16 or wider, within the bound.
A program may use at most 128 MiB of HBM per device.

```python
import math
import jax
import jax.numpy as jnp
import numpy as np
from jax import lax

D = 2048
FF = 4096
SEG_LEN = 16
SEG_DEV = 32
REPLAY_DEV = 32
TOK_DEV = 512
SEGMENTS = 128
TOKENS = 2048
REPLAY = 128
CAP = 16
N_DP = 4


def draw_priorities(key, part):
    key = jax.random.fold_in(key, 7)
    shard_count = REPLAY // REPLAY_DEV
    shard_of = jnp.arange(REPLAY, dtype=jnp.int32) // REPLAY_DEV
    lowest = 16 + 32 * shard_of // max(shard_count - 1, 1)
    values = jax.random.randint(key, (REPLAY,), lowest, 4 * lowest)
    values = values.at[0].set(16).at[REPLAY - 1].set(191)
    return values.astype(jnp.int32)


def plant(drawn, rng, smallest, high):
    longest = drawn.shape.index(max(drawn.shape))
    spots = []
    for shift in (0, 1):
        where = [jax.random.randint(jax.random.fold_in(rng, axis), (), 0, length) for axis, length in enumerate(drawn.shape)]
        where[longest] = (where[longest] + shift) % drawn.shape[longest]
        spots.append(tuple(where))
    return drawn.at[spots[0]].set(smallest).at[spots[1]].set(high)


def raised(result, own_key, source, target, shards_of, factor):
    def block_of(axis_at):
        return (jnp.arange(result.shape[axis_at]) // (result.shape[axis_at] // shards_of)).reshape((-1,) + (1,) * (result.ndim - 1 - axis_at))

    near = jax.random.permutation(own_key, shards_of)[block_of(target)]
    second = (block_of(target) + shards_of // 2) % shards_of
    return jnp.where((block_of(source) == near) | (block_of(source) == second), factor * result, result)


def levels(key, shape, shards, least, high):
    level, own = 1.0, jax.random.fold_in(key, 6)
    for position, parts in shards:
        draws = jnp.exp(jax.random.uniform(jax.random.fold_in(own, position), (parts,), jnp.float32, least / len(shards), high / len(shards)))
        level = level * jnp.repeat(draws, shape[position] // parts).reshape([-1 if axis == position else 1 for axis in range(len(shape))])
    return level


def routed_block(rng, own, number, rows, number_of, top, most, slope):
    order = jax.random.permutation(rng, number_of)
    packed, ordinary = portions_of(number_of, rows * top, most, slope, True), portions_of(number_of, rows * top, most, slope, False)
    places = jnp.arange(number_of)

    def named(sizes, offset_by):
        used = int((sizes > 0).sum())
        fixed = max(1, used // 4)
        moved = fixed + (places - fixed + offset_by * (used - fixed)) % max(1, number_of - fixed)
        return jnp.zeros((number_of,), jnp.int32).at[order[jnp.where(places < fixed, places, moved)]].set(jnp.asarray(sizes, jnp.int32))

    sizes = jnp.where(number % 4 == 0, named(packed, number // 4), named(ordinary, number - number // 4 - 1))
    mixed = jax.random.permutation(jax.random.fold_in(own, 3), number_of)
    giver, receiver = mixed[0:number_of // 2 * 2:2], mixed[1:number_of // 2 * 2:2]
    room = jnp.minimum(sizes[giver] - 1, most - sizes[receiver]) // 2
    room = jnp.where((giver == order[0]) | (receiver == order[0]) | (sizes[receiver] == 0), 0, jnp.maximum(room, 0))
    moved = jax.random.randint(jax.random.fold_in(own, 4), (number_of // 2,), 0, 1 << 20) % (room + 1)
    sizes = sizes.at[giver].add(-moved).at[receiver].add(moved)
    items = jnp.searchsorted(jnp.cumsum(sizes), jnp.arange(rows * top), side="right").astype(jnp.int32)
    listing = items.reshape(top, rows).T
    listing = listing[jax.random.permutation(jax.random.fold_in(own, 1), rows)]
    offset_by = jax.random.randint(jax.random.fold_in(own, 2), (rows, 1), 0, top)
    return jnp.take_along_axis(listing, (jnp.arange(top)[None, :] + offset_by) % top, axis=1)


def portions_of(count, total, limit, slope, full):
    weights = [(1 << 20) // math.isqrt(rank ** slope) + 1 for rank in range(1, count + 1)]
    largest = limit if full else min(limit, max(-(-total // count), total * weights[0] // sum(weights)))
    least = 1 if total - largest >= count - 1 else 0
    given, rest = [largest] + [least] * (count - 1), total - largest - least * (count - 1)
    while rest > 0:
        free = [i for i in range(1, count) if given[i] < largest] or [i for i in range(1, count) if given[i] < limit]
        whole, left = sum([weights[i] for i in free]), rest
        for i in free:
            more = min(limit - given[i], max(1, left * weights[i] // whole), rest)
            given[i] = given[i] + more
            rest = rest - more
    return np.array(given)


def scatter_about(own_key, dims, scale, most, cuts=(), held_as=jnp.bfloat16):
    gain = levels(own_key, dims, cuts, -0.22, 0.18) if cuts else 1.0
    entries = jax.random.normal(own_key, dims, jnp.float32) * scale * gain
    return jnp.minimum(jnp.maximum(entries, -most), most).astype(held_as)


def bell_draw_with(key, extent, deviation, limit, shards, heavy, kind=jnp.bfloat16):
    result = deviation * jax.random.normal(key, extent, jnp.float32)
    if shards:
        result = result * levels(key, extent, shards, -0.22, 0.18)
    return jnp.clip(raised(result, jax.random.fold_in(key, 3), *heavy), -limit, limit).astype(kind)


def setup_inputs(seed: int = 0, part: int = 0) -> dict:
    splits = jax.random.split(jax.random.key(seed), 9)
    own_keys = jax.random.split(jax.random.fold_in(splits[8], part), 9)
    replay_obs = scatter_about(own_keys[0], (REPLAY, SEG_LEN, D), 1.0, 6.0, ((0, 4), (2, 4)))
    priorities = draw_priorities(jax.random.fold_in(jax.random.fold_in(splits[8], part), 71), part)
    sample_owner_keys = jax.random.split(jax.random.fold_in(own_keys[2], 1), SEGMENTS // SEG_DEV)
    sample_owner_turns = jax.random.permutation(jax.random.fold_in(own_keys[2], 3), SEGMENTS // SEG_DEV)
    sample_owner = jax.vmap(lambda own, number: routed_block(jax.random.fold_in(own_keys[2], 2), own, number, SEG_DEV, N_DP, 1, CAP, 2))(sample_owner_keys, sample_owner_turns).reshape((SEGMENTS, 1))
    sample_slot = plant(jax.random.randint(own_keys[3], (SEGMENTS,), 0, REPLAY_DEV), jax.random.fold_in(own_keys[3], 1), 0, REPLAY_DEV - 1).astype(jnp.int32)
    cotangent = bell_draw_with(own_keys[4], (TOKENS, D), (3.0 * TOKENS ** -0.5), 0.39648438, ((0, 4), (1, 4)), (0, 1, 4, 2.0))
    norm_gain = jnp.clip(1.0 + 0.1 * jax.random.normal(splits[5], (D,), jnp.float32), 0.5, 1.5)
    w_in = scatter_about(splits[6], (D, FF), D ** -0.5, 0.125, ((1, 4),))
    w_out = scatter_about(splits[7], (D, FF), FF ** -0.5, 0.09375, ((1, 4),))
    return dict(replay_obs=replay_obs, priorities=priorities, sample_owner=sample_owner, sample_slot=sample_slot, cotangent=cotangent, norm_gain=norm_gain, w_in=w_in, w_out=w_out)


priority_exponent = 0.6
norm_epsilon = 1e-05
root_two_over_pi = 0.7978845608028654

def gelu_tanh(inputs):
    inner = root_two_over_pi * (inputs + 0.044715 * inputs * inputs * inputs)
    return 0.5 * inputs * (1.0 + jnp.tanh(inner))

def gelu_slope(inputs):
    inner = root_two_over_pi * (inputs + 0.044715 * inputs * inputs * inputs)
    tangent = jnp.tanh(inner)
    return 0.5 * (1.0 + tangent) + 0.5 * inputs * (1.0 - tangent * tangent) * root_two_over_pi * (1.0 + 3.0 * 0.044715 * inputs * inputs)

def contract_rows(left, right):
    return lax.dot_general(left, right, (((0,), (0,)), ((), ())), preferred_element_type=jnp.float32)

def reference(replay_obs, priorities, sample_owner, sample_slot, cotangent, norm_gain, w_in, w_out):
    index = (sample_owner[:, 0] * REPLAY_DEV + sample_slot).astype(jnp.int32)
    observed = jnp.take(replay_obs, index, axis=0).reshape(N_DP, TOK_DEV, D)
    raw_weight = jnp.power(jnp.take(priorities, index).astype(jnp.float32), -priority_exponent)
    largest = jnp.max(raw_weight)
    token_weight = jnp.repeat(raw_weight, SEG_LEN).reshape(N_DP, TOK_DEV)
    cot_blocks = cotangent.reshape(N_DP, TOK_DEV, D)

    def learner_block(carry, block):
        obs_block, cot_block, weight_block = block
        inputs32 = obs_block.astype(jnp.float32)
        mean_square = lax.optimization_barrier(jnp.mean(inputs32 * inputs32, axis=1, keepdims=True))
        normed = (inputs32 * lax.rsqrt(mean_square + norm_epsilon) * norm_gain).astype(jnp.bfloat16)
        pre_act = jnp.dot(normed, w_in, preferred_element_type=jnp.float32)
        hidden = gelu_tanh(pre_act).astype(jnp.bfloat16)
        upstream = (cot_block.astype(jnp.float32) * weight_block[:, None]).astype(jnp.bfloat16)
        d_hidden = jnp.dot(upstream, w_out, preferred_element_type=jnp.float32)
        d_pre = (d_hidden * gelu_slope(pre_act)).astype(jnp.bfloat16)
        part_in = lax.optimization_barrier(contract_rows(normed, d_pre).astype(jnp.bfloat16))
        part_out = lax.optimization_barrier(contract_rows(upstream, hidden).astype(jnp.bfloat16))
        return ((carry[0] + part_in.astype(jnp.float32), carry[1] + part_out.astype(jnp.float32)), None)
    start = (jnp.zeros((D, FF), jnp.float32), jnp.zeros((D, FF), jnp.float32))
    (sum_in, sum_out), _ = lax.scan(learner_block, start, (observed, cot_blocks, token_weight))
    return ((sum_in / largest).astype(jnp.bfloat16), (sum_out / largest).astype(jnp.bfloat16))
```

```python
import functools

import jax
import jax.numpy as jnp
from jax import lax
from jax.experimental import pallas as pl
from jax.experimental.pallas import tpu as pltpu
from jax.sharding import PartitionSpec as P

MESH = pl.DeviceIdType.MESH

priority_exponent = 0.6
norm_epsilon = 1e-05
root_two_over_pi = 0.7978845608028654


def gelu_tanh(inputs):
    inner = root_two_over_pi * (inputs + 0.044715 * inputs * inputs * inputs)
    return 0.5 * inputs * (1.0 + jnp.tanh(inner))


def gelu_slope(inputs):
    inner = root_two_over_pi * (inputs + 0.044715 * inputs * inputs * inputs)
    tangent = jnp.tanh(inner)
    return 0.5 * (1.0 + tangent) + 0.5 * inputs * (1.0 - tangent * tangent) * root_two_over_pi * (
        1.0 + 3.0 * 0.044715 * inputs * inputs
    )


def contract_rows(left, right):
    return lax.dot_general(
        left, right, (((0,), (0,)), ((), ())), preferred_element_type=jnp.float32
    )


def backward_hidden(upstream, w_out, pre_act):
    d_hidden = jnp.dot(upstream, w_out, preferred_element_type=jnp.float32)
    return (d_hidden * gelu_slope(pre_act)).astype(jnp.bfloat16)


def body(replay_obs, priorities, sample_owner, sample_slot, cotangent, norm_gain, w_in, w_out):
    shards = lax.axis_size("dp")
    owners = sample_owner[:, 0]
    samples = owners.shape[0]
    capacity = max(2, 2 * samples // shards)
    seg_len = replay_obs.shape[1]
    feature_cols = replay_obs.shape[2]
    order = jnp.arange(samples, dtype=jnp.int32)
    earlier = (owners[:, None] == owners[None, :]) & (order[None, :] < order[:, None])
    rank_in = jnp.sum(earlier.astype(jnp.int32), axis=1)
    position = owners * capacity + rank_in
    table = jnp.arange(shards * capacity, dtype=jnp.int32)
    hits = position[:, None] == table[None, :]
    requests = jnp.sum(jnp.where(hits, sample_slot[:, None], 0), axis=0).reshape(shards, capacity)
    asked = lax.all_to_all(requests, "dp", split_axis=0, concat_axis=0, tiled=True)
    flat = asked.reshape(-1)
    rows_out = jnp.take(replay_obs, flat, axis=0).reshape(asked.shape + (seg_len, feature_cols))
    level_out = (
        jnp.take(priorities, flat).astype(jnp.float32).astype(jnp.bfloat16).reshape(asked.shape)
    )
    arrived = lax.all_to_all(rows_out, "dp", split_axis=0, concat_axis=0, tiled=True)
    arrived_levels = lax.all_to_all(level_out, "dp", split_axis=0, concat_axis=0, tiled=True)
    observed = jnp.take(arrived.reshape(shards * capacity, seg_len, feature_cols), position, axis=0)
    observed = observed.reshape(samples * seg_len, feature_cols)
    levels = jnp.take(arrived_levels.reshape(-1), position).astype(jnp.float32)
    raw_weight = jnp.power(levels, -priority_exponent)
    largest = lax.pmax(jnp.max(raw_weight), "dp")
    whole_obs, whole_cot = (
        lax.all_gather(observed, "mp", axis=1, tiled=True),
        lax.all_gather(cotangent, "mp", axis=1, tiled=True),
    )
    inputs32 = whole_obs.astype(jnp.float32)
    mean_square = jnp.mean(inputs32 * inputs32, axis=1, keepdims=True)
    normed = (inputs32 * lax.rsqrt(mean_square + norm_epsilon) * norm_gain).astype(jnp.bfloat16)
    pre_act = jnp.dot(normed, w_in, preferred_element_type=jnp.float32)
    hidden = gelu_tanh(pre_act).astype(jnp.bfloat16)
    token_weight = jnp.repeat(raw_weight, seg_len)
    upstream = (whole_cot.astype(jnp.float32) * token_weight[:, None]).astype(jnp.bfloat16)
    hidden_cols = w_in.shape[1]
    d_pre = backward_hidden(upstream, w_out, pre_act)
    term_in = contract_rows(normed, d_pre)
    summed = lax.psum_scatter(
        jnp.concatenate([term_in, contract_rows(upstream, hidden)], axis=1).astype(jnp.bfloat16),
        "dp",
        scatter_dimension=0,
        tiled=True,
    ).astype(jnp.float32)
    grad_in_sum = summed[:, :hidden_cols]
    grad_out_sum = summed[:, hidden_cols:]
    return (
        (grad_in_sum / largest).astype(jnp.bfloat16),
        (grad_out_sum / largest).astype(jnp.bfloat16),
    )


SHARDS = 4
PARTS = 4
LEAD = 2
OWNER_AT, SLOT_AT, LEVEL_AT = 0, 32, 64


def gather_kernel(
    chunk, seg_len, meta_ref, gain_ref, obs_ref, cot_ref, win_ref, wout_ref, gin_ref, gout_ref,
    buf, win, wout, hidden_r, slope_r, normed_r, hidden_g, slope_g, normed_g, normed_t, wt,
    acc_in, acc_out, meta_all, weight_v, meta_s, weight_s,
    local_sem, meta_send, meta_recv, zr_send, zl_send, z_recv, x_send, x_recv, c1_send, c1_recv,
    c2_send, c2_recv,
):
    rows, cols = obs_ref.shape
    pieces = rows // chunk
    segs = rows // seg_len
    chunk_segs = chunk // seg_len
    events = 2 * SHARDS * pieces
    half = events // 2
    width = win.shape[1]
    g, z, m = lax.axis_index("groups"), lax.axis_index("dp"), lax.axis_index("mp")
    core, across = m % 2, m // 2
    mate = 2 * across + (1 - core)
    far = 2 * (1 - across) + core
    mate_far = 2 * (1 - across) + (1 - core)
    toward = 1 - 2 * (z // 2)
    inner = ((z + 1) // 2) % 2

    def split(e):
        return e // half, (e // pieces) % SHARDS, e % pieces

    def shard_at(k):
        return z + toward * (k - inner * (k // 2) * (3 - 2 * (k % 2)))

    def block(a, s, c, column):
        return buf.at[
            a,
            pl.ds(pl.multiple_of(s * rows + c * chunk, chunk), chunk),
            pl.ds(pl.multiple_of(column * cols, cols), cols),
        ]

    def move(a, s, c, column, send, recv, target):
        at = (a * SHARDS + s) * pieces + c
        part = block(a, s, c, column)
        return pltpu.make_async_remote_copy(
            src_ref=part, dst_ref=part, send_sem=send.at[at], recv_sem=recv.at[at],
            device_id=target, device_id_type=MESH,
        )

    def along(a, s, c, step):
        return move(a, s, c, m, zr_send if step > 0 else zl_send, z_recv, (g, z + step, m))

    def over_x(a, s, c, column):
        return move(a, s, c, column, x_send, x_recv, (g, z, far))

    def to_mate(a, s, c, column):
        return move(a, s, c, column, c1_send, c1_recv, (g, z, mate))

    def pass_on(a, s, c, column):
        return move(a, s, c, column, c2_send, c2_recv, (g, z, mate))

    def inside(s):
        return jnp.logical_and(s >= 0, s < SHARDS)

    def launch(e):
        a, k, c = split(e)
        for step in (1, -1):
            s = z - step * k

            @pl.when(jnp.logical_and(inside(s), k > 0))
            def _():
                along(a, s, c, step).wait_recv()

            @pl.when(jnp.logical_and(inside(s), inside(z + step)))
            def _():
                along(a, s, c, step).start()

        s = shard_at(k)
        over_x(a, s, c, m).start()
        to_mate(a, s, c, m).start()

    def finish(e):
        a, k, c = split(e)
        for step in (1, -1):
            s = z - step * k

            @pl.when(jnp.logical_and(inside(s), inside(z + step)))
            def _():
                along(a, s, c, step).wait_send()

        s = shard_at(k)
        over_x(a, s, c, m).wait_send()
        to_mate(a, s, c, m).wait_send()
        pass_on(a, s, c, far).wait_send()

    def arrive(e):
        a, k, c = split(e)
        s = shard_at(k)
        over_x(a, s, c, far).wait_recv()
        pass_on(a, s, c, far).start()
        to_mate(a, s, c, mate).wait_recv()
        pass_on(a, s, c, mate_far).wait_recv()
        return s, c

    own_rows = pl.ds(pl.multiple_of(z * rows, rows), rows)
    own_cols = pl.ds(pl.multiple_of(m * cols, cols), cols)
    out_cols = pl.ds(pl.multiple_of(z * cols, cols), cols)
    local = [
        pltpu.make_async_copy(obs_ref, buf.at[0, own_rows, own_cols], local_sem.at[0]),
        pltpu.make_async_copy(cot_ref, buf.at[1, own_rows, own_cols], local_sem.at[1]),
        pltpu.make_async_copy(win_ref, win, local_sem.at[2]),
        pltpu.make_async_copy(wout_ref, wout, local_sem.at[3]),
    ]
    for copy in local:
        copy.start()

    barrier = pltpu.get_barrier_semaphore()
    for target in [(g, (z + d) % SHARDS, m) for d in range(1, SHARDS)] + [(g, z, mate), (g, z, far)]:
        pl.semaphore_signal(barrier, inc=1, device_id=target, device_id_type=MESH)
    pl.semaphore_wait(barrier, SHARDS + 1)

    def tell(d, source):
        return pltpu.make_async_remote_copy(
            src_ref=meta_ref, dst_ref=meta_all.at[source], send_sem=meta_send.at[d - 1],
            recv_sem=meta_recv.at[source], device_id=(g, (z + d) % SHARDS, m), device_id_type=MESH,
        )

    for d in range(1, SHARDS):
        tell(d, z).start()
    local[0].wait()
    local[1].wait()
    for e in range(LEAD):
        launch(jnp.int32(e))
    meta_all[z] = meta_ref[...]
    acc_in[...] = jnp.zeros_like(acc_in)
    acc_out[...] = jnp.zeros_like(acc_out)
    for d in range(1, SHARDS):
        tell(d, (z + SHARDS - d) % SHARDS).wait_recv()
    weight_v[...] = jnp.exp(-priority_exponent * jnp.log(meta_all[...].astype(jnp.float32)))
    for copy in (
        pltpu.make_async_copy(meta_all, meta_s, local_sem.at[4]),
        pltpu.make_async_copy(weight_v, weight_s, local_sem.at[5]),
    ):
        copy.start()
        copy.wait()
    local[2].wait()
    local[3].wait()

    def forward(e, carry):
        launch(e + LEAD)
        s, c = arrive(e)
        first = pl.multiple_of(s * rows + c * chunk, chunk)
        for j in range(chunk_segs):
            weight = weight_s[s, 0, LEVEL_AT + c * chunk_segs + j]
            wt[j * seg_len : (j + 1) * seg_len, :] = jnp.full((seg_len, 128), weight, jnp.float32)

        def norm(t, carry):
            at = pl.multiple_of(t * 64, 64)
            x = buf[0, pl.ds(first + at, 64), :].astype(jnp.float32)
            scale = lax.rsqrt(jnp.mean(x * x, axis=1, keepdims=True) + norm_epsilon)
            normed_t[pl.ds(at, 64), :] = (x * scale * gain_ref[...]).astype(jnp.bfloat16)
            return carry

        lax.fori_loop(0, chunk // 64, norm, 0)
        seg0 = s * segs + c * chunk_segs
        normed_r[pl.ds(seg0, chunk_segs)] = normed_t[:, out_cols].reshape(chunk_segs, seg_len, cols)

        def tile(n, carry):
            at = pl.ds(pl.multiple_of(n * 256, 256), 256)
            u = jnp.dot(normed_t[...], win[:, at], preferred_element_type=jnp.float32)
            weight = wt[:, :1]
            square = u * u
            tangent = jnp.tanh(root_two_over_pi * u * (1.0 + 0.044715 * square))
            upper = 0.5 * weight * (1.0 + tangent)
            slope = upper * (
                1.0 + u * (1.0 - tangent) * (root_two_over_pi * (1.0 + 3.0 * 0.044715 * square))
            )
            hidden = (upper * u).astype(jnp.bfloat16)
            hidden_r[pl.ds(seg0, chunk_segs), :, at] = hidden.reshape(chunk_segs, seg_len, 256)
            slope_r[pl.ds(seg0, chunk_segs), :, at] = slope.reshape(chunk_segs, seg_len, 256)
            return carry

        lax.fori_loop(0, width // 256, tile, 0)
        return carry

    lax.fori_loop(0, half, forward, 0)

    def widest(i, best):
        b, j = i // segs, i % segs
        return jnp.maximum(
            best, weight_s[meta_s[b, 0, OWNER_AT + j], 0, LEVEL_AT + meta_s[b, 0, SLOT_AT + j]]
        )

    largest = lax.fori_loop(0, SHARDS * segs, widest, jnp.float32(0.0))

    def backward(e, carry):
        @pl.when(e + LEAD < events)
        def _():
            launch(e + LEAD)

        _, k, c0 = split(e)
        s0 = shard_at(k)

        def pick(j, carry):
            at = c0 * chunk_segs + j
            r = meta_s[s0, 0, OWNER_AT + at] * segs + meta_s[s0, 0, SLOT_AT + at]
            hidden_g[j] = hidden_r[r]
            slope_g[j] = slope_r[r]
            normed_g[j] = normed_r[r]
            return carry

        lax.fori_loop(0, chunk_segs, pick, 0)
        s, c = arrive(e)
        first = pl.multiple_of(s * rows + c * chunk, chunk)
        here = pl.ds(first, chunk)
        turned = normed_g[...].reshape(chunk, cols).T
        cot_turned = buf[1, here, out_cols].T

        def tile(n, carry):
            at = pl.ds(pl.multiple_of(n * 256, 256), 256)
            d_hidden = jnp.dot(buf[1, here, :], wout[:, at], preferred_element_type=jnp.float32)
            d_pre = (d_hidden * slope_g[:, :, at].reshape(chunk, 256)).astype(jnp.bfloat16)
            acc_in[:, at] += jnp.dot(turned, d_pre, preferred_element_type=jnp.float32)
            acc_out[:, at] += jnp.dot(
                cot_turned, hidden_g[:, :, at].reshape(chunk, 256),
                preferred_element_type=jnp.float32,
            )
            return carry

        lax.fori_loop(0, width // 256, tile, 0)
        return carry

    lax.fori_loop(half, events, backward, 0)
    gin_ref[...] = (acc_in[...] / largest).astype(jnp.bfloat16)
    gout_ref[...] = (acc_out[...] / largest).astype(jnp.bfloat16)

    def settle(e, carry):
        finish(e)
        return carry

    lax.fori_loop(0, events, settle, 0)
    for d in range(1, SHARDS):
        tell(d, z).wait_send()


def gathered_body(
    replay_obs, priorities, sample_owner, sample_slot, cotangent, norm_gain, w_in, w_out
):
    segs, seg_len, cols = replay_obs.shape
    rows = segs * seg_len
    depth, width = w_in.shape
    chunk = 256
    count = 2 * SHARDS * (rows // chunk)
    chunk_segs = chunk // seg_len
    meta = jnp.concatenate(
        [sample_owner[:, 0], sample_slot, priorities, jnp.ones((32,), jnp.int32)]
    )
    meta = jnp.broadcast_to(meta[None, :], (8, 128))
    anywhere = pl.BlockSpec(memory_space=pl.ANY)
    vmem = pl.BlockSpec(memory_space=pltpu.VMEM)
    bf16, f32 = jnp.bfloat16, jnp.float32
    total = SHARDS * segs
    return pl.pallas_call(
        functools.partial(gather_kernel, chunk, seg_len),
        out_shape=[jax.ShapeDtypeStruct((cols, width), bf16)] * 2,
        in_specs=[vmem, vmem, anywhere, anywhere, anywhere, anywhere],
        out_specs=[vmem, vmem],
        scratch_shapes=[
            pltpu.VMEM((2, SHARDS * rows, depth), bf16),
            pltpu.VMEM((depth, width), bf16),
            pltpu.VMEM((depth, width), bf16),
            pltpu.VMEM((total, seg_len, width), bf16),
            pltpu.VMEM((total, seg_len, width), f32),
            pltpu.VMEM((total, seg_len, cols), bf16),
            pltpu.VMEM((chunk_segs, seg_len, width), bf16),
            pltpu.VMEM((chunk_segs, seg_len, width), f32),
            pltpu.VMEM((chunk_segs, seg_len, cols), bf16),
            pltpu.VMEM((chunk, depth), bf16),
            pltpu.VMEM((chunk, 128), f32),
            pltpu.VMEM((cols, width), f32),
            pltpu.VMEM((cols, width), f32),
            pltpu.VMEM((SHARDS, 8, 128), jnp.int32),
            pltpu.VMEM((SHARDS, 8, 128), f32),
            pltpu.SMEM((SHARDS, 8, 128), jnp.int32),
            pltpu.SMEM((SHARDS, 8, 128), f32),
            pltpu.SemaphoreType.DMA((6,)),
            pltpu.SemaphoreType.DMA((SHARDS - 1,)),
            pltpu.SemaphoreType.DMA((SHARDS,)),
        ]
        + [pltpu.SemaphoreType.DMA((count,))] * 9,
        compiler_params=pltpu.CompilerParams(
            collective_id=0, has_side_effects=True, vmem_limit_bytes=58 * 1024 * 1024
        ),
        name="gathered_step",
    )(meta, norm_gain[None, :], replay_obs.reshape(rows, cols), cotangent, w_in, w_out)


def solution(mesh):
    fits = mesh.shape["dp"] == SHARDS and mesh.shape["mp"] == PARTS
    return jax.shard_map(
        gathered_body if fits else body,
        mesh=mesh,
        in_specs=(
            P(("groups", "dp"), None, "mp"),
            P(("groups", "dp")),
            P(("groups", "dp"), None),
            P(("groups", "dp")),
            P(("groups", "dp"), "mp"),
            P(),
            P(None, "mp"),
            P(None, "mp"),
        ),
        out_specs=(P(("groups", "dp"), "mp"), P(("groups", "dp"), "mp")),
        check_vma=False,
    )
```

```python
import functools

import jax
import jax.numpy as jnp
from jax import lax
from jax.experimental import pallas as pl
from jax.experimental.pallas import tpu as pltpu
from jax.sharding import PartitionSpec as P

MESH = pl.DeviceIdType.MESH

priority_exponent = 0.6
norm_epsilon = 1e-05
root_two_over_pi = 0.7978845608028654


def gelu_tanh(inputs):
    inner = root_two_over_pi * (inputs + 0.044715 * inputs * inputs * inputs)
    return 0.5 * inputs * (1.0 + jnp.tanh(inner))


def gelu_slope(inputs):
    inner = root_two_over_pi * (inputs + 0.044715 * inputs * inputs * inputs)
    tangent = jnp.tanh(inner)
    return 0.5 * (1.0 + tangent) + 0.5 * inputs * (1.0 - tangent * tangent) * root_two_over_pi * (
        1.0 + 3.0 * 0.044715 * inputs * inputs
    )


def contract_rows(left, right):
    return lax.dot_general(
        left, right, (((0,), (0,)), ((), ())), preferred_element_type=jnp.float32
    )


def backward_hidden(upstream, w_out, pre_act):
    d_hidden = jnp.dot(upstream, w_out, preferred_element_type=jnp.float32)
    return (d_hidden * gelu_slope(pre_act)).astype(jnp.bfloat16)


def body(replay_obs, priorities, sample_owner, sample_slot, cotangent, norm_gain, w_in, w_out):
    shards = lax.axis_size("dp")
    owners = sample_owner[:, 0]
    samples = owners.shape[0]
    capacity = max(2, 2 * samples // shards)
    seg_len = replay_obs.shape[1]
    feature_cols = replay_obs.shape[2]
    order = jnp.arange(samples, dtype=jnp.int32)
    earlier = (owners[:, None] == owners[None, :]) & (order[None, :] < order[:, None])
    rank_in = jnp.sum(earlier.astype(jnp.int32), axis=1)
    position = owners * capacity + rank_in
    table = jnp.arange(shards * capacity, dtype=jnp.int32)
    hits = position[:, None] == table[None, :]
    requests = jnp.sum(jnp.where(hits, sample_slot[:, None], 0), axis=0).reshape(shards, capacity)
    asked = lax.all_to_all(requests, "dp", split_axis=0, concat_axis=0, tiled=True)
    flat = asked.reshape(-1)
    rows_out = jnp.take(replay_obs, flat, axis=0).reshape(asked.shape + (seg_len, feature_cols))
    level_out = (
        jnp.take(priorities, flat).astype(jnp.float32).astype(jnp.bfloat16).reshape(asked.shape)
    )
    arrived = lax.all_to_all(rows_out, "dp", split_axis=0, concat_axis=0, tiled=True)
    arrived_levels = lax.all_to_all(level_out, "dp", split_axis=0, concat_axis=0, tiled=True)
    observed = jnp.take(arrived.reshape(shards * capacity, seg_len, feature_cols), position, axis=0)
    observed = observed.reshape(samples * seg_len, feature_cols)
    levels = jnp.take(arrived_levels.reshape(-1), position).astype(jnp.float32)
    raw_weight = jnp.power(levels, -priority_exponent)
    largest = lax.pmax(jnp.max(raw_weight), "dp")
    whole_obs, whole_cot = (
        lax.all_gather(observed, "mp", axis=1, tiled=True),
        lax.all_gather(cotangent, "mp", axis=1, tiled=True),
    )
    inputs32 = whole_obs.astype(jnp.float32)
    mean_square = jnp.mean(inputs32 * inputs32, axis=1, keepdims=True)
    normed = (inputs32 * lax.rsqrt(mean_square + norm_epsilon) * norm_gain).astype(jnp.bfloat16)
    pre_act = jnp.dot(normed, w_in, preferred_element_type=jnp.float32)
    hidden = gelu_tanh(pre_act).astype(jnp.bfloat16)
    token_weight = jnp.repeat(raw_weight, seg_len)
    upstream = (whole_cot.astype(jnp.float32) * token_weight[:, None]).astype(jnp.bfloat16)
    hidden_cols = w_in.shape[1]
    d_pre = backward_hidden(upstream, w_out, pre_act)
    term_in = contract_rows(normed, d_pre)
    summed = lax.psum_scatter(
        jnp.concatenate([term_in, contract_rows(upstream, hidden)], axis=1).astype(jnp.bfloat16),
        "dp",
        scatter_dimension=0,
        tiled=True,
    ).astype(jnp.float32)
    grad_in_sum = summed[:, :hidden_cols]
    grad_out_sum = summed[:, hidden_cols:]
    return (
        (grad_in_sum / largest).astype(jnp.bfloat16),
        (grad_out_sum / largest).astype(jnp.bfloat16),
    )


SHARDS = 4
PARTS = 4
LEAD = 2
OWNER_AT, SLOT_AT, LEVEL_AT = 0, 32, 64


def gather_kernel(
    chunk, seg_len, meta_ref, gain_ref, obs_ref, cot_ref, win_ref, wout_ref, gin_ref, gout_ref,
    buf, win, wout, hidden_r, slope_r, normed_r, hidden_g, slope_g, normed_g, normed_t, wt,
    acc_in, acc_out, meta_all, weight_v, meta_s, weight_s,
    local_sem, meta_send, meta_recv, zr_send, zl_send, z_recv, x_send, x_recv, c1_send, c1_recv,
    c2_send, c2_recv,
):
    rows, cols = obs_ref.shape
    pieces = rows // chunk
    segs = rows // seg_len
    chunk_segs = chunk // seg_len
    events = 2 * SHARDS * pieces
    half = events // 2
    width = win.shape[1]
    g, z, m = lax.axis_index("groups"), lax.axis_index("dp"), lax.axis_index("mp")
    core, across = m % 2, m // 2
    mate = 2 * across + (1 - core)
    far = 2 * (1 - across) + core
    mate_far = 2 * (1 - across) + (1 - core)
    toward = 1 - 2 * (z // 2)
    inner = ((z + 1) // 2) % 2

    def split(e):
        return e // half, (e // pieces) % SHARDS, e % pieces

    def shard_at(k):
        return z + toward * (k - inner * (k // 2) * (3 - 2 * (k % 2)))

    def block(a, s, c, column):
        return buf.at[
            a,
            pl.ds(pl.multiple_of(s * rows + c * chunk, chunk), chunk),
            pl.ds(pl.multiple_of(column * cols, cols), cols),
        ]

    def move(a, s, c, column, send, recv, target):
        at = (a * SHARDS + s) * pieces + c
        part = block(a, s, c, column)
        return pltpu.make_async_remote_copy(
            src_ref=part, dst_ref=part, send_sem=send.at[at], recv_sem=recv.at[at],
            device_id=target, device_id_type=MESH,
        )

    def along(a, s, c, step):
        return move(a, s, c, m, zr_send if step > 0 else zl_send, z_recv, (g, z + step, m))

    def over_x(a, s, c, column):
        return move(a, s, c, column, x_send, x_recv, (g, z, far))

    def to_mate(a, s, c, column):
        return move(a, s, c, column, c1_send, c1_recv, (g, z, mate))

    def pass_on(a, s, c, column):
        return move(a, s, c, column, c2_send, c2_recv, (g, z, mate))

    def inside(s):
        return jnp.logical_and(s >= 0, s < SHARDS)

    def launch(e):
        a, k, c = split(e)
        for step in (1, -1):
            s = z - step * k

            @pl.when(jnp.logical_and(inside(s), k > 0))
            def _():
                along(a, s, c, step).wait_recv()

            @pl.when(jnp.logical_and(inside(s), inside(z + step)))
            def _():
                along(a, s, c, step).start()

        s = shard_at(k)
        over_x(a, s, c, m).start()
        to_mate(a, s, c, m).start()

    def finish(e):
        a, k, c = split(e)
        for step in (1, -1):
            s = z - step * k

            @pl.when(jnp.logical_and(inside(s), inside(z + step)))
            def _():
                along(a, s, c, step).wait_send()

        s = shard_at(k)
        over_x(a, s, c, m).wait_send()
        to_mate(a, s, c, m).wait_send()
        pass_on(a, s, c, far).wait_send()

    def arrive(e):
        a, k, c = split(e)
        s = shard_at(k)
        over_x(a, s, c, far).wait_recv()
        pass_on(a, s, c, far).start()
        to_mate(a, s, c, mate).wait_recv()
        pass_on(a, s, c, mate_far).wait_recv()
        return s, c

    own_rows = pl.ds(pl.multiple_of(z * rows, rows), rows)
    own_cols = pl.ds(pl.multiple_of(m * cols, cols), cols)
    out_cols = pl.ds(pl.multiple_of(z * cols, cols), cols)
    local = [
        pltpu.make_async_copy(obs_ref, buf.at[0, own_rows, own_cols], local_sem.at[0]),
        pltpu.make_async_copy(cot_ref, buf.at[1, own_rows, own_cols], local_sem.at[1]),
        pltpu.make_async_copy(win_ref, win, local_sem.at[2]),
        pltpu.make_async_copy(wout_ref, wout, local_sem.at[3]),
    ]
    for copy in local:
        copy.start()

    barrier = pltpu.get_barrier_semaphore()
    for target in [(g, (z + d) % SHARDS, m) for d in range(1, SHARDS)] + [(g, z, mate), (g, z, far)]:
        pl.semaphore_signal(barrier, inc=1, device_id=target, device_id_type=MESH)
    pl.semaphore_wait(barrier, SHARDS + 1)

    def tell(d, source):
        return pltpu.make_async_remote_copy(
            src_ref=meta_ref, dst_ref=meta_all.at[source], send_sem=meta_send.at[d - 1],
            recv_sem=meta_recv.at[source], device_id=(g, (z + d) % SHARDS, m), device_id_type=MESH,
        )

    for d in range(1, SHARDS):
        tell(d, z).start()
    local[0].wait()
    local[1].wait()
    for e in range(LEAD):
        launch(jnp.int32(e))
    meta_all[z] = meta_ref[...]
    acc_in[...] = jnp.zeros_like(acc_in)
    acc_out[...] = jnp.zeros_like(acc_out)
    for d in range(1, SHARDS):
        tell(d, (z + SHARDS - d) % SHARDS).wait_recv()
    weight_v[...] = jnp.exp(-priority_exponent * jnp.log(meta_all[...].astype(jnp.float32)))
    for copy in (
        pltpu.make_async_copy(meta_all, meta_s, local_sem.at[4]),
        pltpu.make_async_copy(weight_v, weight_s, local_sem.at[5]),
    ):
        copy.start()
        copy.wait()
    local[2].wait()
    local[3].wait()

    def forward(e, carry):
        launch(e + LEAD)
        s, c = arrive(e)
        first = pl.multiple_of(s * rows + c * chunk, chunk)
        for j in range(chunk_segs):
            weight = weight_s[s, 0, LEVEL_AT + c * chunk_segs + j]
            wt[j * seg_len : (j + 1) * seg_len, :] = jnp.full((seg_len, 128), weight, jnp.float32)

        def norm(t, carry):
            at = pl.multiple_of(t * 64, 64)
            x = buf[0, pl.ds(first + at, 64), :].astype(jnp.float32)
            scale = lax.rsqrt(jnp.mean(x * x, axis=1, keepdims=True) + norm_epsilon)
            normed_t[pl.ds(at, 64), :] = (x * scale * gain_ref[...]).astype(jnp.bfloat16)
            return carry

        lax.fori_loop(0, chunk // 64, norm, 0)
        seg0 = s * segs + c * chunk_segs
        normed_r[pl.ds(seg0, chunk_segs)] = normed_t[:, out_cols].reshape(chunk_segs, seg_len, cols)

        def tile(n, carry):
            at = pl.ds(pl.multiple_of(n * 512, 512), 512)
            u = jnp.dot(normed_t[...], win[:, at], preferred_element_type=jnp.float32)
            weight = wt[:, :1]
            square = u * u
            tangent = jnp.tanh(root_two_over_pi * u * (1.0 + 0.044715 * square))
            upper = 0.5 * weight * (1.0 + tangent)
            slope = upper * (
                1.0 + u * (1.0 - tangent) * (root_two_over_pi * (1.0 + 3.0 * 0.044715 * square))
            )
            hidden = (upper * u).astype(jnp.bfloat16)
            hidden_r[pl.ds(seg0, chunk_segs), :, at] = hidden.reshape(chunk_segs, seg_len, 512)
            slope_r[pl.ds(seg0, chunk_segs), :, at] = slope.reshape(chunk_segs, seg_len, 512)
            return carry

        lax.fori_loop(0, width // 512, tile, 0)
        return carry

    lax.fori_loop(0, half, forward, 0)

    def widest(i, best):
        b, j = i // segs, i % segs
        return jnp.maximum(
            best, weight_s[meta_s[b, 0, OWNER_AT + j], 0, LEVEL_AT + meta_s[b, 0, SLOT_AT + j]]
        )

    largest = lax.fori_loop(0, SHARDS * segs, widest, jnp.float32(0.0))

    def backward(e, carry):
        @pl.when(e + LEAD < events)
        def _():
            launch(e + LEAD)

        _, k, c0 = split(e)
        s0 = shard_at(k)

        def pick(j, carry):
            at = c0 * chunk_segs + j
            r = meta_s[s0, 0, OWNER_AT + at] * segs + meta_s[s0, 0, SLOT_AT + at]
            hidden_g[j] = hidden_r[r]
            slope_g[j] = slope_r[r]
            normed_g[j] = normed_r[r]
            return carry

        lax.fori_loop(0, chunk_segs, pick, 0)
        s, c = arrive(e)
        first = pl.multiple_of(s * rows + c * chunk, chunk)
        here = pl.ds(first, chunk)
        turned = normed_g[...].reshape(chunk, cols).T
        cot_turned = buf[1, here, out_cols].T

        def tile(n, carry):
            at = pl.ds(pl.multiple_of(n * 512, 512), 512)
            d_hidden = jnp.dot(buf[1, here, :], wout[:, at], preferred_element_type=jnp.float32)
            d_pre = (d_hidden * slope_g[:, :, at].reshape(chunk, 512)).astype(jnp.bfloat16)
            acc_in[:, at] += jnp.dot(turned, d_pre, preferred_element_type=jnp.float32)
            acc_out[:, at] += jnp.dot(
                cot_turned, hidden_g[:, :, at].reshape(chunk, 512),
                preferred_element_type=jnp.float32,
            )
            return carry

        lax.fori_loop(0, width // 512, tile, 0)
        return carry

    lax.fori_loop(half, events, backward, 0)
    gin_ref[...] = (acc_in[...] / largest).astype(jnp.bfloat16)
    gout_ref[...] = (acc_out[...] / largest).astype(jnp.bfloat16)

    def settle(e, carry):
        finish(e)
        return carry

    lax.fori_loop(0, events, settle, 0)
    for d in range(1, SHARDS):
        tell(d, z).wait_send()


def gathered_body(
    replay_obs, priorities, sample_owner, sample_slot, cotangent, norm_gain, w_in, w_out
):
    segs, seg_len, cols = replay_obs.shape
    rows = segs * seg_len
    depth, width = w_in.shape
    chunk = 256
    count = 2 * SHARDS * (rows // chunk)
    chunk_segs = chunk // seg_len
    meta = jnp.concatenate(
        [sample_owner[:, 0], sample_slot, priorities, jnp.ones((32,), jnp.int32)]
    )
    meta = jnp.broadcast_to(meta[None, :], (8, 128))
    anywhere = pl.BlockSpec(memory_space=pl.ANY)
    vmem = pl.BlockSpec(memory_space=pltpu.VMEM)
    bf16, f32 = jnp.bfloat16, jnp.float32
    total = SHARDS * segs
    return pl.pallas_call(
        functools.partial(gather_kernel, chunk, seg_len),
        out_shape=[jax.ShapeDtypeStruct((cols, width), bf16)] * 2,
        in_specs=[vmem, vmem, anywhere, anywhere, anywhere, anywhere],
        out_specs=[vmem, vmem],
        scratch_shapes=[
            pltpu.VMEM((2, SHARDS * rows, depth), bf16),
            pltpu.VMEM((depth, width), bf16),
            pltpu.VMEM((depth, width), bf16),
            pltpu.VMEM((total, seg_len, width), bf16),
            pltpu.VMEM((total, seg_len, width), f32),
            pltpu.VMEM((total, seg_len, cols), bf16),
            pltpu.VMEM((chunk_segs, seg_len, width), bf16),
            pltpu.VMEM((chunk_segs, seg_len, width), f32),
            pltpu.VMEM((chunk_segs, seg_len, cols), bf16),
            pltpu.VMEM((chunk, depth), bf16),
            pltpu.VMEM((chunk, 128), f32),
            pltpu.VMEM((cols, width), f32),
            pltpu.VMEM((cols, width), f32),
            pltpu.VMEM((SHARDS, 8, 128), jnp.int32),
            pltpu.VMEM((SHARDS, 8, 128), f32),
            pltpu.SMEM((SHARDS, 8, 128), jnp.int32),
            pltpu.SMEM((SHARDS, 8, 128), f32),
            pltpu.SemaphoreType.DMA((6,)),
            pltpu.SemaphoreType.DMA((SHARDS - 1,)),
            pltpu.SemaphoreType.DMA((SHARDS,)),
        ]
        + [pltpu.SemaphoreType.DMA((count,))] * 9,
        compiler_params=pltpu.CompilerParams(
            collective_id=0, has_side_effects=True, vmem_limit_bytes=58 * 1024 * 1024
        ),
        name="gathered_step",
    )(meta, norm_gain[None, :], replay_obs.reshape(rows, cols), cotangent, w_in, w_out)


def solution(mesh):
    fits = mesh.shape["dp"] == SHARDS and mesh.shape["mp"] == PARTS
    return jax.shard_map(
        gathered_body if fits else body,
        mesh=mesh,
        in_specs=(
            P(("groups", "dp"), None, "mp"),
            P(("groups", "dp")),
            P(("groups", "dp"), None),
            P(("groups", "dp")),
            P(("groups", "dp"), "mp"),
            P(),
            P(None, "mp"),
            P(None, "mp"),
        ),
        out_specs=(P(("groups", "dp"), "mp"), P(("groups", "dp"), "mp")),
        check_vma=False,
    )
```

```python
import functools

import jax
import jax.numpy as jnp
from jax import lax
from jax.experimental import pallas as pl
from jax.experimental.pallas import tpu as pltpu
from jax.sharding import PartitionSpec as P

MESH = pl.DeviceIdType.MESH

priority_exponent = 0.6
norm_epsilon = 1e-05
root_two_over_pi = 0.7978845608028654


def gelu_tanh(inputs):
    inner = root_two_over_pi * (inputs + 0.044715 * inputs * inputs * inputs)
    return 0.5 * inputs * (1.0 + jnp.tanh(inner))


def gelu_slope(inputs):
    inner = root_two_over_pi * (inputs + 0.044715 * inputs * inputs * inputs)
    tangent = jnp.tanh(inner)
    return 0.5 * (1.0 + tangent) + 0.5 * inputs * (1.0 - tangent * tangent) * root_two_over_pi * (
        1.0 + 3.0 * 0.044715 * inputs * inputs
    )


def contract_rows(left, right):
    return lax.dot_general(
        left, right, (((0,), (0,)), ((), ())), preferred_element_type=jnp.float32
    )


def backward_hidden(upstream, w_out, pre_act):
    d_hidden = jnp.dot(upstream, w_out, preferred_element_type=jnp.float32)
    return (d_hidden * gelu_slope(pre_act)).astype(jnp.bfloat16)


def body(replay_obs, priorities, sample_owner, sample_slot, cotangent, norm_gain, w_in, w_out):
    shards = lax.axis_size("dp")
    owners = sample_owner[:, 0]
    samples = owners.shape[0]
    capacity = max(2, 2 * samples // shards)
    seg_len = replay_obs.shape[1]
    feature_cols = replay_obs.shape[2]
    order = jnp.arange(samples, dtype=jnp.int32)
    earlier = (owners[:, None] == owners[None, :]) & (order[None, :] < order[:, None])
    rank_in = jnp.sum(earlier.astype(jnp.int32), axis=1)
    position = owners * capacity + rank_in
    table = jnp.arange(shards * capacity, dtype=jnp.int32)
    hits = position[:, None] == table[None, :]
    requests = jnp.sum(jnp.where(hits, sample_slot[:, None], 0), axis=0).reshape(shards, capacity)
    asked = lax.all_to_all(requests, "dp", split_axis=0, concat_axis=0, tiled=True)
    flat = asked.reshape(-1)
    rows_out = jnp.take(replay_obs, flat, axis=0).reshape(asked.shape + (seg_len, feature_cols))
    level_out = (
        jnp.take(priorities, flat).astype(jnp.float32).astype(jnp.bfloat16).reshape(asked.shape)
    )
    arrived = lax.all_to_all(rows_out, "dp", split_axis=0, concat_axis=0, tiled=True)
    arrived_levels = lax.all_to_all(level_out, "dp", split_axis=0, concat_axis=0, tiled=True)
    observed = jnp.take(arrived.reshape(shards * capacity, seg_len, feature_cols), position, axis=0)
    observed = observed.reshape(samples * seg_len, feature_cols)
    levels = jnp.take(arrived_levels.reshape(-1), position).astype(jnp.float32)
    raw_weight = jnp.power(levels, -priority_exponent)
    largest = lax.pmax(jnp.max(raw_weight), "dp")
    whole_obs, whole_cot = (
        lax.all_gather(observed, "mp", axis=1, tiled=True),
        lax.all_gather(cotangent, "mp", axis=1, tiled=True),
    )
    inputs32 = whole_obs.astype(jnp.float32)
    mean_square = jnp.mean(inputs32 * inputs32, axis=1, keepdims=True)
    normed = (inputs32 * lax.rsqrt(mean_square + norm_epsilon) * norm_gain).astype(jnp.bfloat16)
    pre_act = jnp.dot(normed, w_in, preferred_element_type=jnp.float32)
    hidden = gelu_tanh(pre_act).astype(jnp.bfloat16)
    token_weight = jnp.repeat(raw_weight, seg_len)
    upstream = (whole_cot.astype(jnp.float32) * token_weight[:, None]).astype(jnp.bfloat16)
    hidden_cols = w_in.shape[1]
    d_pre = backward_hidden(upstream, w_out, pre_act)
    term_in = contract_rows(normed, d_pre)
    summed = lax.psum_scatter(
        jnp.concatenate([term_in, contract_rows(upstream, hidden)], axis=1).astype(jnp.bfloat16),
        "dp",
        scatter_dimension=0,
        tiled=True,
    ).astype(jnp.float32)
    grad_in_sum = summed[:, :hidden_cols]
    grad_out_sum = summed[:, hidden_cols:]
    return (
        (grad_in_sum / largest).astype(jnp.bfloat16),
        (grad_out_sum / largest).astype(jnp.bfloat16),
    )


SHARDS = 4
PARTS = 4
LEAD = 2
OWNER_AT, SLOT_AT, LEVEL_AT = 0, 32, 64


def gather_kernel(
    chunk, seg_len, meta_ref, gain_ref, obs_ref, cot_ref, win_ref, wout_ref, gin_ref, gout_ref,
    buf, win, wout, hidden_r, slope_r, normed_r, hidden_g, slope_g, normed_g, normed_t, wt,
    acc_in, acc_out, meta_all, weight_v, meta_s, weight_s,
    local_sem, meta_send, meta_recv, zr_send, zl_send, z_recv, x_send, x_recv, c1_send, c1_recv,
    c2_send, c2_recv,
):
    rows, cols = obs_ref.shape
    pieces = rows // chunk
    segs = rows // seg_len
    chunk_segs = chunk // seg_len
    events = 2 * SHARDS * pieces
    half = events // 2
    width = win.shape[1]
    g, z, m = lax.axis_index("groups"), lax.axis_index("dp"), lax.axis_index("mp")
    core, across = m % 2, m // 2
    mate = 2 * across + (1 - core)
    far = 2 * (1 - across) + core
    mate_far = 2 * (1 - across) + (1 - core)
    toward = 1 - 2 * (z // 2)
    inner = ((z + 1) // 2) % 2

    def split(e):
        return e // half, (e // pieces) % SHARDS, e % pieces

    def shard_at(k):
        return z + toward * (k - inner * (k // 2) * (3 - 2 * (k % 2)))

    def block(a, s, c, column):
        return buf.at[
            a,
            pl.ds(pl.multiple_of(s * rows + c * chunk, chunk), chunk),
            pl.ds(pl.multiple_of(column * cols, cols), cols),
        ]

    def move(a, s, c, column, send, recv, target):
        at = (a * SHARDS + s) * pieces + c
        part = block(a, s, c, column)
        return pltpu.make_async_remote_copy(
            src_ref=part, dst_ref=part, send_sem=send.at[at], recv_sem=recv.at[at],
            device_id=target, device_id_type=MESH,
        )

    def along(a, s, c, step):
        return move(a, s, c, m, zr_send if step > 0 else zl_send, z_recv, (g, z + step, m))

    def over_x(a, s, c, column):
        return move(a, s, c, column, x_send, x_recv, (g, z, far))

    def to_mate(a, s, c, column):
        return move(a, s, c, column, c1_send, c1_recv, (g, z, mate))

    def pass_on(a, s, c, column):
        return move(a, s, c, column, c2_send, c2_recv, (g, z, mate))

    def inside(s):
        return jnp.logical_and(s >= 0, s < SHARDS)

    def launch(e):
        a, k, c = split(e)
        for step in (1, -1):
            s = z - step * k

            @pl.when(jnp.logical_and(inside(s), k > 0))
            def _():
                along(a, s, c, step).wait_recv()

            @pl.when(jnp.logical_and(inside(s), inside(z + step)))
            def _():
                along(a, s, c, step).start()

        s = shard_at(k)
        over_x(a, s, c, m).start()
        to_mate(a, s, c, m).start()

    def finish(e):
        a, k, c = split(e)
        for step in (1, -1):
            s = z - step * k

            @pl.when(jnp.logical_and(inside(s), inside(z + step)))
            def _():
                along(a, s, c, step).wait_send()

        s = shard_at(k)
        over_x(a, s, c, m).wait_send()
        to_mate(a, s, c, m).wait_send()
        pass_on(a, s, c, far).wait_send()

    def arrive(e):
        a, k, c = split(e)
        s = shard_at(k)
        over_x(a, s, c, far).wait_recv()
        pass_on(a, s, c, far).start()
        to_mate(a, s, c, mate).wait_recv()
        pass_on(a, s, c, mate_far).wait_recv()
        return s, c

    own_rows = pl.ds(pl.multiple_of(z * rows, rows), rows)
    own_cols = pl.ds(pl.multiple_of(m * cols, cols), cols)
    out_cols = pl.ds(pl.multiple_of(z * cols, cols), cols)
    local = [
        pltpu.make_async_copy(obs_ref, buf.at[0, own_rows, own_cols], local_sem.at[0]),
        pltpu.make_async_copy(cot_ref, buf.at[1, own_rows, own_cols], local_sem.at[1]),
        pltpu.make_async_copy(win_ref, win, local_sem.at[2]),
        pltpu.make_async_copy(wout_ref, wout, local_sem.at[3]),
    ]
    for copy in local:
        copy.start()

    barrier = pltpu.get_barrier_semaphore()
    for target in [(g, (z + d) % SHARDS, m) for d in range(1, SHARDS)] + [(g, z, mate), (g, z, far)]:
        pl.semaphore_signal(barrier, inc=1, device_id=target, device_id_type=MESH)
    pl.semaphore_wait(barrier, SHARDS + 1)

    def tell(d, source):
        return pltpu.make_async_remote_copy(
            src_ref=meta_ref, dst_ref=meta_all.at[source], send_sem=meta_send.at[d - 1],
            recv_sem=meta_recv.at[source], device_id=(g, (z + d) % SHARDS, m), device_id_type=MESH,
        )

    for d in range(1, SHARDS):
        tell(d, z).start()
    local[0].wait()
    local[1].wait()
    for e in range(LEAD):
        launch(jnp.int32(e))
    meta_all[z] = meta_ref[...]
    acc_in[...] = jnp.zeros_like(acc_in)
    acc_out[...] = jnp.zeros_like(acc_out)
    for d in range(1, SHARDS):
        tell(d, (z + SHARDS - d) % SHARDS).wait_recv()
    weight_v[...] = jnp.exp(-priority_exponent * jnp.log(meta_all[...].astype(jnp.float32)))
    for copy in (
        pltpu.make_async_copy(meta_all, meta_s, local_sem.at[4]),
        pltpu.make_async_copy(weight_v, weight_s, local_sem.at[5]),
    ):
        copy.start()
        copy.wait()
    local[2].wait()
    local[3].wait()

    def forward(e, carry):
        launch(e + LEAD)
        s, c = arrive(e)
        first = pl.multiple_of(s * rows + c * chunk, chunk)
        for j in range(chunk_segs):
            weight = weight_s[s, 0, LEVEL_AT + c * chunk_segs + j]
            wt[j * seg_len : (j + 1) * seg_len, :] = jnp.full((seg_len, 128), weight, jnp.float32)

        def norm(t, carry):
            at = pl.multiple_of(t * 64, 64)
            x = buf[0, pl.ds(first + at, 64), :].astype(jnp.float32)
            scale = lax.rsqrt(jnp.mean(x * x, axis=1, keepdims=True) + norm_epsilon)
            normed_t[pl.ds(at, 64), :] = (x * scale * gain_ref[...]).astype(jnp.bfloat16)
            return carry

        lax.fori_loop(0, chunk // 64, norm, 0)
        seg0 = s * segs + c * chunk_segs
        normed_r[pl.ds(seg0, chunk_segs)] = normed_t[:, out_cols].reshape(chunk_segs, seg_len, cols)

        def tile(n, carry):
            at = pl.ds(pl.multiple_of(n * 1024, 1024), 1024)
            u = jnp.dot(normed_t[...], win[:, at], preferred_element_type=jnp.float32)
            weight = wt[:, :1]
            square = u * u
            tangent = jnp.tanh(root_two_over_pi * u * (1.0 + 0.044715 * square))
            upper = 0.5 * weight * (1.0 + tangent)
            slope = upper * (
                1.0 + u * (1.0 - tangent) * (root_two_over_pi * (1.0 + 3.0 * 0.044715 * square))
            )
            hidden = (upper * u).astype(jnp.bfloat16)
            hidden_r[pl.ds(seg0, chunk_segs), :, at] = hidden.reshape(chunk_segs, seg_len, 1024)
            slope_r[pl.ds(seg0, chunk_segs), :, at] = slope.reshape(chunk_segs, seg_len, 1024)
            return carry

        lax.fori_loop(0, width // 1024, tile, 0)
        return carry

    lax.fori_loop(0, half, forward, 0)

    def widest(i, best):
        b, j = i // segs, i % segs
        return jnp.maximum(
            best, weight_s[meta_s[b, 0, OWNER_AT + j], 0, LEVEL_AT + meta_s[b, 0, SLOT_AT + j]]
        )

    largest = lax.fori_loop(0, SHARDS * segs, widest, jnp.float32(0.0))

    def backward(e, carry):
        @pl.when(e + LEAD < events)
        def _():
            launch(e + LEAD)

        _, k, c0 = split(e)
        s0 = shard_at(k)

        def pick(j, carry):
            at = c0 * chunk_segs + j
            r = meta_s[s0, 0, OWNER_AT + at] * segs + meta_s[s0, 0, SLOT_AT + at]
            hidden_g[j] = hidden_r[r]
            slope_g[j] = slope_r[r]
            normed_g[j] = normed_r[r]
            return carry

        lax.fori_loop(0, chunk_segs, pick, 0)
        s, c = arrive(e)
        first = pl.multiple_of(s * rows + c * chunk, chunk)
        here = pl.ds(first, chunk)
        turned = normed_g[...].reshape(chunk, cols).T
        cot_turned = buf[1, here, out_cols].T

        def tile(n, carry):
            at = pl.ds(pl.multiple_of(n * 1024, 1024), 1024)
            d_hidden = jnp.dot(buf[1, here, :], wout[:, at], preferred_element_type=jnp.float32)
            d_pre = (d_hidden * slope_g[:, :, at].reshape(chunk, 1024)).astype(jnp.bfloat16)
            acc_in[:, at] += jnp.dot(turned, d_pre, preferred_element_type=jnp.float32)
            acc_out[:, at] += jnp.dot(
                cot_turned, hidden_g[:, :, at].reshape(chunk, 1024),
                preferred_element_type=jnp.float32,
            )
            return carry

        lax.fori_loop(0, width // 1024, tile, 0)
        return carry

    lax.fori_loop(half, events, backward, 0)
    inverse = 1.0 / jnp.full((1, 128), largest, jnp.float32)[:, :1]
    gin_ref[...] = (acc_in[...] * inverse).astype(jnp.bfloat16)
    gout_ref[...] = (acc_out[...] * inverse).astype(jnp.bfloat16)

    def settle(e, carry):
        finish(e)
        return carry

    lax.fori_loop(0, events, settle, 0)
    for d in range(1, SHARDS):
        tell(d, z).wait_send()


def gathered_body(
    replay_obs, priorities, sample_owner, sample_slot, cotangent, norm_gain, w_in, w_out
):
    segs, seg_len, cols = replay_obs.shape
    rows = segs * seg_len
    depth, width = w_in.shape
    chunk = 256
    count = 2 * SHARDS * (rows // chunk)
    chunk_segs = chunk // seg_len
    meta = jnp.concatenate(
        [sample_owner[:, 0], sample_slot, priorities, jnp.ones((32,), jnp.int32)]
    )
    meta = jnp.broadcast_to(meta[None, :], (8, 128))
    anywhere = pl.BlockSpec(memory_space=pl.ANY)
    vmem = pl.BlockSpec(memory_space=pltpu.VMEM)
    bf16, f32 = jnp.bfloat16, jnp.float32
    total = SHARDS * segs
    return pl.pallas_call(
        functools.partial(gather_kernel, chunk, seg_len),
        out_shape=[jax.ShapeDtypeStruct((cols, width), bf16)] * 2,
        in_specs=[vmem, vmem, anywhere, anywhere, anywhere, anywhere],
        out_specs=[vmem, vmem],
        scratch_shapes=[
            pltpu.VMEM((2, SHARDS * rows, depth), bf16),
            pltpu.VMEM((depth, width), bf16),
            pltpu.VMEM((depth, width), bf16),
            pltpu.VMEM((total, seg_len, width), bf16),
            pltpu.VMEM((total, seg_len, width), f32),
            pltpu.VMEM((total, seg_len, cols), bf16),
            pltpu.VMEM((chunk_segs, seg_len, width), bf16),
            pltpu.VMEM((chunk_segs, seg_len, width), f32),
            pltpu.VMEM((chunk_segs, seg_len, cols), bf16),
            pltpu.VMEM((chunk, depth), bf16),
            pltpu.VMEM((chunk, 128), f32),
            pltpu.VMEM((cols, width), f32),
            pltpu.VMEM((cols, width), f32),
            pltpu.VMEM((SHARDS, 8, 128), jnp.int32),
            pltpu.VMEM((SHARDS, 8, 128), f32),
            pltpu.SMEM((SHARDS, 8, 128), jnp.int32),
            pltpu.SMEM((SHARDS, 8, 128), f32),
            pltpu.SemaphoreType.DMA((6,)),
            pltpu.SemaphoreType.DMA((SHARDS - 1,)),
            pltpu.SemaphoreType.DMA((SHARDS,)),
        ]
        + [pltpu.SemaphoreType.DMA((count,))] * 9,
        compiler_params=pltpu.CompilerParams(
            collective_id=0, has_side_effects=True, vmem_limit_bytes=58 * 1024 * 1024
        ),
        name="gathered_step",
    )(meta, norm_gain[None, :], replay_obs.reshape(rows, cols), cotangent, w_in, w_out)


def solution(mesh):
    fits = mesh.shape["dp"] == SHARDS and mesh.shape["mp"] == PARTS
    return jax.shard_map(
        gathered_body if fits else body,
        mesh=mesh,
        in_specs=(
            P(("groups", "dp"), None, "mp"),
            P(("groups", "dp")),
            P(("groups", "dp"), None),
            P(("groups", "dp")),
            P(("groups", "dp"), "mp"),
            P(),
            P(None, "mp"),
            P(None, "mp"),
        ),
        out_specs=(P(("groups", "dp"), "mp"), P(("groups", "dp"), "mp")),
        check_vma=False,
    )
```
